512 devices in a mesh: pp: 8 (over x, y_lo), cp: 64 (over y_hi, z, core).
Axes of the slice: x: 4, y: 8 (y_hi: 4, y_lo: 2; y = y_hi * 2 + y_lo), z: 8, core: 2. Of those that a mesh axis runs over, the one named last changes fastest.
Arguments:
- queries: bfloat16 [8, 2, 32, 4096, 128], P('pp', None, None, 'cp'), may hold values from -5 to 5
- keys_values: bfloat16 [8, 2, 2, 4, 4096, 128], P('pp', None, None, None, 'cp'), may hold values from -5 to 5
- old_block: int32 [128], replicated, may hold values from 0 to 127, as said below
- new_block: int32 [128], replicated, may hold values from 0 to 127, as said below
Outputs:
- section_input: bfloat16 [8, 2, 32, 4096, 128], P('pp', None, None, 'cp')
The draws below stay inside these ranges and needn't reach their ends.
Inputs may be any that keep to these rules, and one draw needn't show every extreme that they name: `old_block`: A permutation of the sequence blocks; row-blocks 4 e to 4 e + 3 hold sequence blocks 2 a, 2 a + 1, 2 b, 2 b + 1 with a + b = 63. `new_block`: A permutation of the sequence blocks; row-blocks 2 d and 2 d + 1 hold sequence blocks c and 127 - c.
All inputs are finite; a program needn't handle non-finite values.
Results may differ from the reference program's by a relative error of at most 0.0098.
Values may be sent and summed in bfloat16 or wider, within the bound.
A program may use at most 64 MiB of HBM per device.

```python
import math
import jax
import jax.numpy as jnp
from jax import lax

SEQUENCES = 2
QUERY_HEADS = 32
KV_HEADS = 4
HEAD_DIM = 128
SECTIONS = 8
BLOCKS = 128
LENGTH = 4096


def draw_queries(key, part):
    key = jax.random.fold_in(key, 1)
    full_shape = (SECTIONS, SEQUENCES, QUERY_HEADS, LENGTH, HEAD_DIM)
    drawn = jnp.clip(jax.random.normal(key, full_shape, jnp.float32), -5.0, 5.0)
    return drawn.astype(jnp.bfloat16)


def draw_keys_values(key, part):
    key = jax.random.fold_in(key, 2)
    full_shape = (SECTIONS, 2, SEQUENCES, KV_HEADS, LENGTH, HEAD_DIM)
    drawn = jnp.clip(jax.random.normal(key, full_shape, jnp.float32), -5.0, 5.0)
    return drawn.astype(jnp.bfloat16)


def draw_old_block(key, part):
    key = jax.random.fold_in(key, 5)
    shuffled = jax.random.permutation(key, BLOCKS // 4).astype(jnp.int32)
    paired = jnp.stack([shuffled, BLOCKS // 2 - 1 - shuffled], axis=1)
    blocks_out = 2 * paired[:, :, None] + jnp.arange(2, dtype=jnp.int32)[None, None, :]
    return blocks_out.reshape(BLOCKS).astype(jnp.int32)


def draw_new_block(key, part):
    key = jax.random.fold_in(key, 7)
    shuffled = jax.random.permutation(key, BLOCKS // 2).astype(jnp.int32)
    flipped = jax.random.randint(jax.random.fold_in(key, 1), (BLOCKS // 2,), 0, 2)
    leading = jnp.where(flipped == 1, BLOCKS - 1 - shuffled, shuffled)
    trailing = BLOCKS - 1 - leading
    return jnp.stack([leading, trailing], axis=1).reshape(BLOCKS).astype(jnp.int32)


def setup_inputs(seed: int = 0) -> dict:
    keys = jax.random.split(jax.random.key(seed), 5)
    return {
        "queries": draw_queries(jax.random.fold_in(keys[4], 71), 0),
        "keys_values": draw_keys_values(jax.random.fold_in(keys[4], 71), 0),
        "old_block": draw_old_block(jax.random.fold_in(keys[4], 71), 0),
        "new_block": draw_new_block(jax.random.fold_in(keys[4], 71), 0),
    }


def regroup(tensor, block_order):
    dims_shape = tensor.shape
    count_blocks = block_order.shape[0]
    blocked = tensor.reshape(dims_shape[:-2] + (count_blocks, dims_shape[-2] // count_blocks, dims_shape[-1]))
    picked = jnp.take(blocked, block_order, axis=blocked.ndim - 3)
    return picked.reshape(dims_shape)

def rotate(tensor):
    half_dim = tensor.shape[-1] // 2
    spacing = jnp.arange(half_dim, dtype=jnp.float32) * (2.0 / tensor.shape[-1])
    inverse = jnp.exp(-spacing * jnp.log(jnp.float32(1000000.0)))
    angles = jnp.arange(tensor.shape[-2], dtype=jnp.float32)[:, None] * inverse[None, :]
    cosine = jnp.cos(angles)
    sine_part = jnp.sin(angles)
    widened = tensor.astype(jnp.float32)
    first_half = widened[..., :half_dim]
    second_half = widened[..., half_dim:]
    turned = jnp.concatenate([first_half * cosine - second_half * sine_part, second_half * cosine + first_half * sine_part], axis=-1)
    return turned.astype(jnp.bfloat16)

def attend(query_seq, key_seq, value_seq):
    group_size = QUERY_HEADS // KV_HEADS
    block_rows = min(512, LENGTH)
    score_scale = 1.0 / math.sqrt(HEAD_DIM)
    grouped = query_seq.reshape(SEQUENCES, KV_HEADS, group_size, LENGTH, HEAD_DIM)
    outputs = []
    for first_row in range(0, LENGTH, block_rows):
        finish = first_row + block_rows
        query_part = grouped[:, :, :, first_row:finish].astype(jnp.float32)
        key_part = key_seq[:, :, :finish].astype(jnp.float32)
        value_part = value_seq[:, :, :finish].astype(jnp.float32)
        scores = jnp.einsum('sgqrd,sgkd->sgqrk', query_part, key_part, precision=lax.Precision.HIGHEST) * score_scale
        allowed = jnp.arange(finish)[None, :] <= (first_row + jnp.arange(block_rows))[:, None]
        scores = jnp.where(allowed, scores, -jnp.inf)
        highest = lax.optimization_barrier(jnp.max(scores, axis=-1, keepdims=True))
        weights = jnp.exp(scores - highest)
        weight_sum = lax.optimization_barrier(jnp.sum(weights, axis=-1, keepdims=True))
        rounded = lax.optimization_barrier(weights.astype(jnp.bfloat16)).astype(jnp.float32)
        blended = jnp.einsum('sgqrk,sgkd->sgqrd', rounded, value_part, precision=lax.Precision.HIGHEST) / weight_sum
        outputs.append(blended.astype(jnp.bfloat16))
    return jnp.concatenate(outputs, axis=3).reshape(SEQUENCES, QUERY_HEADS, LENGTH, HEAD_DIM)

def reference(queries, keys_values, old_block, new_block):
    positions = jnp.arange(BLOCKS, dtype=jnp.int32)
    inverse = jnp.zeros((BLOCKS,), jnp.int32).at[old_block].set(positions)

    def one_section(operands):
        section_queries, section_pairs = operands
        query_seq = rotate(regroup(section_queries, inverse))
        key_seq = rotate(regroup(section_pairs[0], inverse))
        value_seq = regroup(section_pairs[1], inverse)
        attended = attend(query_seq, key_seq, value_seq)
        return regroup(attended, new_block)
    relaid = lax.map(one_section, (queries, keys_values))
    return jnp.roll(relaid, 1, axis=0)
```

```python
import functools
import math
import random

import jax
import jax.numpy as jnp
from jax import lax
from jax.experimental import pallas as pl
from jax.experimental.pallas import tpu as pltpu
from jax.sharding import PartitionSpec as P

MESH = pl.DeviceIdType.MESH
F32 = jnp.float32
BF16 = jnp.bfloat16
LENGTH = 4096
DIM = 128
BLOCKS = 128
ROWS = 32
LOCAL = 64
YS, ZS = 4, 8
SECTIONS = 8
VROWS = 144


def steps_of(seed):
    steps = [(dy, dz, dc) for dy in range(YS) for dz in range(ZS) for dc in range(2)]
    random.Random(seed).shuffle(steps)
    return steps


def place():
    me = lax.axis_index("cp")
    return me // 16, lax.rem(me // 2, ZS), lax.rem(me, 2)


def at(dy, dz, dc):
    y, z, c = place()
    return lax.rem(y + dy, YS) * 16 + lax.rem(z + dz, ZS) * 2 + lax.rem(c + dc, 2)


def turned(x, cos, sin):
    wide = x.astype(F32)
    return (wide * cos + pltpu.roll(wide, 64, wide.ndim - 1) * sin).astype(BF16)


def gather_kernel(
    q_ref, kv_ref, cos_ref, sin_ref, oq_ref, okv_ref, qs, kvs,
    q_send, q_recv, z_send, z_recv, y_send, y_recv, c_send, c_recv, loc,
):
    pp = lax.axis_index("pp")
    me = lax.axis_index("cp")
    y, z, c = place()
    steps = [s for s in steps_of(1) if s != (0, 0, 0)]
    barrier = pltpu.get_barrier_semaphore()
    for s in steps:
        pl.semaphore_signal(barrier, inc=1, device_id=(pp, at(*s)), device_id_type=MESH)
    cos, sin = cos_ref[...], sin_ref[...]

    def turn_keys(j, carry):
        kvs[0, j] = turned(kv_ref[0, j], cos, sin)
        kvs[1, j] = kv_ref[1, j]
        return carry

    lax.fori_loop(0, 8, turn_keys, 0)
    pl.semaphore_wait(barrier, len(steps))

    def remote(src, dst, send, recv, dev):
        copy = pltpu.make_async_remote_copy(
            src_ref=src, dst_ref=dst, send_sem=send, recv_sem=recv,
            device_id=(pp, dev), device_id_type=MESH,
        )
        copy.start()
        return copy

    z_copies = []
    for n, dz in enumerate((4, 3, 5, 2, 6, 1, 7)):
        z_copies.append(remote(
            kvs.at[:, lax.rem(z + dz, ZS)], okv_ref.at[:, y, c, z],
            z_send.at[n], z_recv.at[n], at(0, dz, 0),
        ))
    own = pltpu.make_async_copy(kvs.at[:, z], okv_ref.at[:, y, c, z], loc.at[0])
    own.start()

    q_copies = []

    def send_queries(first, last):
        for n in range(first, last):
            d = at(*steps[n])
            dy, dz, dc = steps[n]
            item = lax.rem(z + dz, ZS) * 8 + lax.rem(y + dy, YS) * 2 + lax.rem(c + dc, 2)
            qs[item] = turned(q_ref[item], cos, sin)
            q_copies.append(remote(qs.at[item], oq_ref.at[me], q_send.at[n], q_recv.at[n], d))

    send_queries(0, 20)
    mine = z * 8 + y * 2 + c
    qs[mine] = turned(q_ref[mine], cos, sin)
    own_q = pltpu.make_async_copy(qs.at[mine], oq_ref.at[me], loc.at[1])
    own_q.start()

    for copy in z_copies:
        copy.wait_recv()
    own.wait()
    mine_kv = okv_ref.at[:, y, c]
    up = remote(mine_kv, mine_kv, y_send.at[0], y_recv.at[0], at(1, 0, 0))
    down = remote(mine_kv, mine_kv, y_send.at[1], y_recv.at[1], at(YS - 1, 0, 0))
    core = [remote(mine_kv, mine_kv, c_send.at[0], c_recv.at[0], at(0, 0, 1))]
    send_queries(20, 42)
    below, above, far = lax.rem(y + 3, YS), lax.rem(y + 1, YS), lax.rem(y + 2, YS)
    up.wait_recv()
    keys = okv_ref.at[0, below, c]
    up2 = remote(keys, keys, y_send.at[2], y_recv.at[2], at(1, 0, 0))
    part = okv_ref.at[:, below, c]
    core.append(remote(part, part, c_send.at[1], c_recv.at[1], at(0, 0, 1)))
    down.wait_recv()
    values = okv_ref.at[1, above, c]
    down2 = remote(values, values, y_send.at[3], y_recv.at[3], at(YS - 1, 0, 0))
    part = okv_ref.at[:, above, c]
    core.append(remote(part, part, c_send.at[2], c_recv.at[2], at(0, 0, 1)))
    send_queries(42, 63)
    up2.wait_recv()
    down2.wait_recv()
    part = okv_ref.at[:, far, c]
    core.append(remote(part, part, c_send.at[3], c_recv.at[3], at(0, 0, 1)))
    own_q.wait()
    for copy in q_copies + core:
        copy.wait()
    for copy in z_copies + [up, down, up2, down2]:
        copy.wait_send()


def gather(queries, pairs, cos, sin):
    vmem = pl.BlockSpec(memory_space=pltpu.VMEM)
    hbm = pl.BlockSpec(memory_space=pl.ANY)
    dma = pltpu.SemaphoreType.DMA
    return pl.pallas_call(
        gather_kernel,
        out_shape=(
            jax.ShapeDtypeStruct((64, LOCAL, DIM), BF16),
            jax.ShapeDtypeStruct((2, YS, 2, ZS, LOCAL, DIM), BF16),
        ),
        in_specs=[vmem] * 4,
        out_specs=(hbm, hbm),
        scratch_shapes=[
            pltpu.VMEM((64, LOCAL, DIM), BF16),
            pltpu.VMEM((2, 8, LOCAL, DIM), BF16),
            dma((63,)), dma((63,)), dma((7,)), dma((7,)), dma((4,)), dma((4,)), dma((4,)), dma((4,)), dma((2,)),
        ],
        compiler_params=pltpu.CompilerParams(
            collective_id=1, has_side_effects=True, vmem_limit_bytes=24 * 2**20
        ),
        name="gather",
    )(queries, pairs, cos, sin)


def scatter_kernel(x_ref, o_ref, send, recv):
    pp = lax.axis_index("pp")
    ahead, behind = lax.rem(pp + 1, SECTIONS), lax.rem(pp + SECTIONS - 1, SECTIONS)
    y, z, c = place()
    item = z * 8 + y * 2 + c
    steps = steps_of(2)
    barrier = pltpu.get_barrier_semaphore()
    for s in steps:
        pl.semaphore_signal(barrier, inc=1, device_id=(behind, at(*s)), device_id_type=MESH)
    pl.semaphore_wait(barrier, len(steps))
    copies = []
    for n, s in enumerate(steps):
        d = at(*s)
        copy = pltpu.make_async_remote_copy(
            src_ref=x_ref.at[d], dst_ref=o_ref.at[item], send_sem=send.at[n], recv_sem=recv.at[n],
            device_id=(ahead, d), device_id_type=MESH,
        )
        copy.start()
        copies.append(copy)
    for copy in copies:
        copy.wait()


def scatter(relaid):
    hbm = pl.BlockSpec(memory_space=pl.ANY)
    return pl.pallas_call(
        scatter_kernel,
        out_shape=jax.ShapeDtypeStruct((64, LOCAL, DIM), BF16),
        in_specs=[hbm],
        out_specs=hbm,
        scratch_shapes=[pltpu.SemaphoreType.DMA((64,)), pltpu.SemaphoreType.DMA((64,))],
        compiler_params=pltpu.CompilerParams(
            collective_id=2, has_side_effects=True, vmem_limit_bytes=24 * 2**20
        ),
        name="scatter",
    )(relaid)


def key_row_block(j):
    device = j // 2
    y, z, c = device // 16, lax.rem(device // 2, ZS), lax.rem(device, 2)
    return ((y * 2 + c) * ZS + z) * 2 + lax.rem(j, 2)


def attend_kernel(old_ref, new_ref, q_ref, kv_ref, o_ref, qs, k2, vt, qt, oseq, acc, mx, *, bq, bk):
    scale = math.log2(math.e) / math.sqrt(DIM)

    def arrange(j, carry):
        dst = pl.ds(pl.multiple_of(old_ref[j] * ROWS, ROWS), ROWS)
        src = pl.ds(pl.multiple_of(key_row_block(j) * ROWS, ROWS), ROWS)
        keys = kv_ref[0, src, :]
        k2[dst, 0:DIM] = keys
        k2[dst, DIM : 2 * DIM] = keys
        qs[dst, :] = q_ref[pl.ds(pl.multiple_of(j * ROWS, ROWS), ROWS), :]
        oseq[dst, :] = kv_ref[1, src, :]
        return carry

    lax.fori_loop(0, BLOCKS, arrange, 0, unroll=8)

    def turn(j, carry):
        rows = pl.ds(pl.multiple_of(j * 512, 512), 512)
        x = qs[rows, :].astype(F32) * scale
        high = x.astype(BF16)
        low = (x - high.astype(F32)).astype(BF16)
        qt[0:DIM, rows] = high.T
        qt[DIM : 2 * DIM, rows] = low.T
        vt[0:DIM, rows] = oseq[rows, :].T
        vt[DIM:VROWS, rows] = jnp.ones((VROWS - DIM, 512), BF16)
        return carry

    lax.fori_loop(0, LENGTH // 512, turn, 0)

    def query_step(i, carry):
        q0 = pl.multiple_of(i * bq, bq)

        def block(k0, width, first):
            s = jnp.dot(k2[pl.ds(k0, width), :], qt[:, pl.ds(q0, bq)], preferred_element_type=F32)
            if first:
                key = lax.broadcasted_iota(jnp.int32, s.shape, 0)
                query = lax.broadcasted_iota(jnp.int32, s.shape, 1)
                s = jnp.where(key <= query, s, -1e30)
            top = jnp.max(s, axis=0, keepdims=True)
            if not first:
                before = mx[...]
                top = jnp.maximum(before, top)
            weights = jnp.exp2(s - top).astype(BF16)
            summed = jnp.dot(vt[:, pl.ds(k0, width)], weights, preferred_element_type=F32)
            if not first:
                summed = acc[...] * jnp.exp2(before - top) + summed
            acc[...] = summed
            mx[...] = top

        block(q0, bq, True)

        def body(j, inner):
            block(pl.multiple_of(j * bk, bk), bk, False)
            return inner

        lax.fori_loop(0, i * bq // bk, body, 0)
        oseq[pl.ds(q0, bq), :] = (acc[0:DIM, :] / acc[DIM : DIM + 1, :]).T.astype(BF16)
        return carry

    lax.fori_loop(0, LENGTH // bq, query_step, 0)

    def relay(j, carry):
        src = pl.ds(pl.multiple_of(new_ref[j] * ROWS, ROWS), ROWS)
        o_ref[pl.ds(pl.multiple_of(j * ROWS, ROWS), ROWS), :] = oseq[src, :]
        return carry

    lax.fori_loop(0, BLOCKS, relay, 0, unroll=8)


def attend(old_block, new_block, queries, pairs, bq=1024, bk=1024):
    vmem = pl.BlockSpec(memory_space=pltpu.VMEM)
    smem = pl.BlockSpec(memory_space=pltpu.SMEM)
    return pl.pallas_call(
        functools.partial(attend_kernel, bq=bq, bk=bk),
        out_shape=jax.ShapeDtypeStruct((LENGTH, DIM), BF16),
        in_specs=[smem, smem, vmem, vmem],
        out_specs=vmem,
        scratch_shapes=[
            pltpu.VMEM((LENGTH, DIM), BF16),
            pltpu.VMEM((LENGTH, 2 * DIM), BF16),
            pltpu.VMEM((VROWS, LENGTH), BF16),
            pltpu.VMEM((2 * DIM, LENGTH), BF16),
            pltpu.VMEM((LENGTH, DIM), BF16),
            pltpu.VMEM((VROWS, bq), F32),
            pltpu.VMEM((1, bq), F32),
        ],
        compiler_params=pltpu.CompilerParams(vmem_limit_bytes=48 * 2**20),
        name="attend",
    )(old_block, new_block, queries, pairs)


def per_device(queries, keys_values, old_block, new_block):
    me = lax.axis_index("cp")
    two = lax.dynamic_slice_in_dim(old_block, me * 2, 2)
    token = (two[:, None] * ROWS + jnp.arange(ROWS, dtype=jnp.int32)[None, :]).reshape(LOCAL)
    spacing = jnp.arange(DIM // 2, dtype=F32) * (2.0 / DIM)
    inverse = jnp.exp(-spacing * jnp.log(F32(1000000.0)))
    angles = token.astype(F32)[:, None] * inverse[None, :]
    cosine, sine = jnp.cos(angles), jnp.sin(angles)
    cos = jnp.concatenate([cosine, cosine], axis=1)
    sin = jnp.concatenate([-sine, sine], axis=1)
    all_queries, pairs = gather(
        queries.reshape(64, LOCAL, DIM), keys_values.reshape(2, 8, LOCAL, DIM), cos, sin
    )
    relaid = attend(
        old_block, new_block, all_queries.reshape(LENGTH, DIM),
        pairs.reshape(2, LENGTH, DIM),
    )
    moved = scatter(relaid.reshape(64, LOCAL, DIM))
    return moved.reshape(queries.shape)


def solution(mesh):
    return jax.shard_map(
        per_device,
        mesh=mesh,
        in_specs=(P("pp", None, None, "cp", None), P("pp", None, None, None, "cp", None), P(), P()),
        out_specs=P("pp", None, None, "cp", None),
        check_vma=False,
    )
```

```python
import math
import random

import jax
import jax.numpy as jnp
from jax import lax
from jax.experimental import pallas as pl
from jax.experimental.pallas import tpu as pltpu
from jax.sharding import PartitionSpec as P

MESH = pl.DeviceIdType.MESH
F32 = jnp.float32
BF16 = jnp.bfloat16
LENGTH = 4096
DIM = 128
BLOCKS = 128
ROWS = 32
LOCAL = 64
YS, ZS = 4, 8
CHIPS = YS * ZS
SECTIONS = 8
VROWS = 144
TILE = 1024
TB = TILE // ROWS


def steps_of(seed):
    rest = [(dy, dz) for dy in range(YS) for dz in range(ZS)]
    random.Random(seed).shuffle(rest)
    hops_y = {0: 0, 1: 2, 2: 4, 3: 2}
    total, order = [0, 0], []
    while rest:
        share = 64 * (len(order) + 1) / 32

        def cost(step):
            along_z = total[0] + min(step[1], ZS - step[1])
            along_y = total[1] + hops_y[step[0]]
            return (along_z - share) ** 2 + (along_y - share) ** 2

        best = min(rest, key=cost)
        rest.remove(best)
        order.append(best)
        total[0] += min(best[1], ZS - best[1])
        total[1] += hops_y[best[0]]
    return order


def turned(x, cos, sin):
    wide = x.astype(F32)
    return (wide * cos + pltpu.roll(wide, 64, wide.ndim - 1) * sin).astype(BF16)


def layer_kernel(
    kv_block, q_block, new_block, q_ref, kv_ref, cos_ref, sin_ref, o_ref,
    qs, kvs, okv, qa, qb, oa, ob, ra, rb, k2, vt, seq, qt, acc, mx,
    q_send, q_recv, z_send, z_recv, y_send, y_recv, c_send, c_recv,
    x_send, x_recv, t_send, t_recv, o_send, o_recv, loc,
):
    pp = lax.axis_index("pp")
    me = lax.axis_index("cp")
    y, z, c = me // 16, lax.rem(me // 2, ZS), lax.rem(me, 2)
    chip = y * ZS + z
    ahead, behind = lax.rem(pp + 1, SECTIONS), lax.rem(pp + SECTIONS - 1, SECTIONS)
    other = 1 - c

    def at(dy, dz, core):
        return (lax.rem(y + dy + YS, YS) * ZS + lax.rem(z + dz + ZS, ZS)) * 2 + core

    sign = 1 - 2 * c

    def mirrored(step):
        return lax.rem(y + sign * step[0] + YS, YS), lax.rem(z + sign * step[1] + ZS, ZS)

    def device(place):
        return (place[0] * ZS + place[1]) * 2 + c

    q_steps = [s for s in steps_of(1) if s != (0, 0)]
    o_steps = steps_of(2)

    barrier = pltpu.get_barrier_semaphore()
    for s in q_steps:
        pl.semaphore_signal(barrier, inc=1, device_id=(pp, device(mirrored(s))), device_id_type=MESH)
    pl.semaphore_signal(barrier, inc=1, device_id=(pp, at(0, 0, other)), device_id_type=MESH)
    for s in o_steps:
        pl.semaphore_signal(barrier, inc=1, device_id=(behind, device(mirrored(s))), device_id_type=MESH)

    cos, sin = cos_ref[...], sin_ref[...]

    def turn_keys(j, carry):
        kvs[0, j] = turned(kv_ref[0, j], cos, sin).reshape(2, ROWS, DIM)
        kvs[1, j] = kv_ref[1, j].reshape(2, ROWS, DIM)
        return carry

    lax.fori_loop(0, 8, turn_keys, 0)
    pl.semaphore_wait(barrier, 64)

    def remote(src, dst, send, recv, dev, section=pp):
        copy = pltpu.make_async_remote_copy(
            src_ref=src, dst_ref=dst, send_sem=send, recv_sem=recv,
            device_id=(section, dev), device_id_type=MESH,
        )
        copy.start()
        return copy

    def plane(at_y):
        return (at_y * 2 + c) * 16

    z_copies = []
    for n, dz in enumerate((4, 3, 5, 2, 6, 1, 7)):
        z_copies.append(remote(
            kvs.at[:, lax.rem(z + dz, ZS)], okv.at[:, pl.ds(plane(y) + 2 * z, 2)],
            z_send.at[n], z_recv.at[n], at(0, dz, c),
        ))
    own = pltpu.make_async_copy(kvs.at[:, z], okv.at[:, pl.ds(plane(y) + 2 * z, 2)], loc.at[0])
    own.start()

    held = (qa, qb)
    slot_of = (c * CHIPS + chip) * 2
    q_copies = ([], [])

    def send_queries(head, first, last):
        for n in range(first, last):
            to = mirrored(q_steps[n])
            item = to[1] * 8 + to[0] * 2 + head
            qs[item] = turned(q_ref[item], cos, sin).reshape(2, ROWS, DIM)
            q_copies[head].append(remote(
                qs.at[item], held[head].at[pl.ds(slot_of, 2)], q_send.at[head, n], q_recv.at[head, n], device(to)
            ))

    def keep_queries(head):
        item = z * 8 + y * 2 + head
        held[head][pl.ds(slot_of, 2)] = turned(q_ref[item], cos, sin).reshape(2, ROWS, DIM)

    send_queries(0, 0, 12)
    keep_queries(0)
    keep_queries(1)
    for copy in z_copies:
        copy.wait_recv()
    own.wait()
    part = okv.at[:, pl.ds(plane(y), 16)]
    up = remote(part, part, y_send.at[0], y_recv.at[0], at(1, 0, c))
    down = remote(part, part, y_send.at[1], y_recv.at[1], at(YS - 1, 0, c))
    core = [remote(part, part, c_send.at[0], c_recv.at[0], at(0, 0, other))]
    send_queries(0, 12, 31)
    below, above, far = lax.rem(y + 3, YS), lax.rem(y + 1, YS), lax.rem(y + 2, YS)
    up.wait_recv()
    keys = okv.at[0, pl.ds(plane(below), 16)]
    up2 = remote(keys, keys, y_send.at[2], y_recv.at[2], at(1, 0, c))
    part = okv.at[:, pl.ds(plane(below), 16)]
    core.append(remote(part, part, c_send.at[1], c_recv.at[1], at(0, 0, other)))
    down.wait_recv()
    values = okv.at[1, pl.ds(plane(above), 16)]
    down2 = remote(values, values, y_send.at[3], y_recv.at[3], at(YS - 1, 0, c))
    part = okv.at[:, pl.ds(plane(above), 16)]
    core.append(remote(part, part, c_send.at[2], c_recv.at[2], at(0, 0, other)))
    send_queries(1, 0, 31)
    up2.wait_recv()
    down2.wait_recv()
    part = okv.at[:, pl.ds(plane(far), 16)]
    core.append(remote(part, part, c_send.at[3], c_recv.at[3], at(0, 0, other)))
    for copy in core:
        copy.wait()
    for copy in z_copies + [up, down, up2, down2]:
        copy.wait_send()

    def arrange(b, carry):
        dst = pl.ds(pl.multiple_of(b * ROWS, ROWS), ROWS)
        keys = okv[0, kv_block[b]]
        k2[dst, 0:DIM] = keys
        k2[dst, DIM : 2 * DIM] = keys
        seq[dst, :] = okv[1, kv_block[b]]
        return carry

    lax.fori_loop(0, BLOCKS, arrange, 0, unroll=8)
    for j in range(LENGTH // 512):
        vt[0:DIM, j * 512 : (j + 1) * 512] = seq[j * 512 : (j + 1) * 512, :].T
    vt[DIM:VROWS, :] = jnp.ones((VROWS - DIM, LENGTH), BF16)

    scale = math.log2(math.e) / math.sqrt(DIM)
    tiles = (c, 3 - c)

    def attend(head, out):
        for copy in q_copies[head]:
            copy.wait_recv()
        mine = held[head].at[pl.ds(c * 2 * CHIPS, 2 * CHIPS)]
        swap = remote(mine, mine, x_send.at[head], x_recv.at[head], at(0, 0, other))
        swap.wait()
        t_copies = []
        for slot in range(2):
            tile = tiles[slot]

            def pick(b, carry):
                seq[pl.ds(pl.multiple_of(b * ROWS, ROWS), ROWS), :] = held[head][q_block[tile * TB + b]]
                return carry

            lax.fori_loop(0, TB, pick, 0, unroll=8)
            for j in range(TILE // 512):
                cols = slice(j * 512, (j + 1) * 512)
                x = seq[cols, :].astype(F32) * scale
                high = x.astype(BF16)
                low = (x - high.astype(F32)).astype(BF16)
                qt[0:DIM, cols] = high.T
                qt[DIM : 2 * DIM, cols] = low.T

            def block(k0, first):
                s = jnp.dot(k2[pl.ds(k0, TILE), :], qt[...], preferred_element_type=F32)
                if first:
                    key = lax.broadcasted_iota(jnp.int32, s.shape, 0)
                    query = lax.broadcasted_iota(jnp.int32, s.shape, 1)
                    s = jnp.where(key <= query, s, -1e30)
                top = jnp.max(s, axis=0, keepdims=True)
                if not first:
                    before = mx[...]
                    top = jnp.maximum(before, top)
                weights = jnp.exp2(s - top).astype(BF16)
                summed = jnp.dot(vt[:, pl.ds(k0, TILE)], weights, preferred_element_type=F32)
                if not first:
                    summed = acc[...] * jnp.exp2(before - top) + summed
                acc[...] = summed
                mx[...] = top

            block(pl.multiple_of(tile * TILE, TILE), True)

            def body(j, carry):
                block(pl.multiple_of(j * TILE, TILE), False)
                return carry

            lax.fori_loop(0, tile, body, 0)
            rows = pl.ds(tile * TB, TB)
            out[rows] = (acc[0:DIM, :] / acc[DIM : DIM + 1, :]).T.astype(BF16).reshape(TB, ROWS, DIM)
            done = out.at[rows]
            t_copies.append(remote(
                done, done, t_send.at[head, slot], t_recv.at[head, slot], at(0, 0, other)
            ))
        for copy in t_copies:
            copy.wait()

    def hand_on(head, out, relaid):
        def relay(b, carry):
            j = (b // 2) * 4 + 2 * c + lax.rem(b, 2)
            relaid[b] = out[new_block[j]]
            return carry

        lax.fori_loop(0, 2 * CHIPS, relay, 0, unroll=8)
        copies = []
        for n, s in enumerate(o_steps):
            to = mirrored(s)
            rows = pl.ds((to[0] * ZS + to[1]) * 2, 2)
            copies.append(remote(
                relaid.at[rows], o_ref.at[z * 8 + y * 2 + head],
                o_send.at[head, n], o_recv.at[head, n], device(to), ahead,
            ))
        return copies

    attend(0, oa)
    o_copies = hand_on(0, oa, ra)
    attend(1, ob)
    o_copies += hand_on(1, ob, rb)
    for copy in q_copies[0] + q_copies[1]:
        copy.wait_send()
    for copy in o_copies:
        copy.wait()


def layer(kv_block, q_block, new_block, queries, pairs, cos, sin):
    vmem = pl.BlockSpec(memory_space=pltpu.VMEM)
    smem = pl.BlockSpec(memory_space=pltpu.SMEM)
    dma = pltpu.SemaphoreType.DMA
    buf = pltpu.VMEM
    return pl.pallas_call(
        layer_kernel,
        out_shape=jax.ShapeDtypeStruct((64, 2, ROWS, DIM), BF16),
        in_specs=[smem] * 3 + [vmem] * 4,
        out_specs=pl.BlockSpec(memory_space=pl.ANY),
        scratch_shapes=[
            buf((64, 2, ROWS, DIM), BF16),
            buf((2, 8, 2, ROWS, DIM), BF16),
            buf((2, BLOCKS, ROWS, DIM), BF16),
            buf((BLOCKS, ROWS, DIM), BF16),
            buf((BLOCKS, ROWS, DIM), BF16),
            buf((BLOCKS, ROWS, DIM), BF16),
            buf((BLOCKS, ROWS, DIM), BF16),
            buf((BLOCKS // 2, ROWS, DIM), BF16),
            buf((BLOCKS // 2, ROWS, DIM), BF16),
            buf((LENGTH, 2 * DIM), BF16),
            buf((VROWS, LENGTH), BF16),
            buf((LENGTH, DIM), BF16),
            buf((2 * DIM, TILE), BF16),
            buf((VROWS, TILE), F32),
            buf((1, TILE), F32),
            dma((2, 31)), dma((2, 31)), dma((7,)), dma((7,)), dma((4,)), dma((4,)), dma((4,)), dma((4,)),
            dma((2,)), dma((2,)), dma((2, 2)), dma((2, 2)), dma((2, 32)), dma((2, 32)), dma((1,)),
        ],
        compiler_params=pltpu.CompilerParams(
            collective_id=1, has_side_effects=True, vmem_limit_bytes=50 * 2**20
        ),
        name="layer",
    )(kv_block, q_block, new_block, queries, pairs, cos, sin)


def per_device(queries, keys_values, old_block, new_block):
    me = lax.axis_index("cp")
    two = lax.dynamic_slice_in_dim(old_block, me * 2, 2)
    token = (two[:, None] * ROWS + jnp.arange(ROWS, dtype=jnp.int32)[None, :]).reshape(LOCAL)
    spacing = jnp.arange(DIM // 2, dtype=F32) * (2.0 / DIM)
    inverse = jnp.exp(-spacing * jnp.log(F32(1000000.0)))
    angles = token.astype(F32)[:, None] * inverse[None, :]
    cosine, sine = jnp.cos(angles), jnp.sin(angles)
    cos = jnp.concatenate([cosine, cosine], axis=1)
    sin = jnp.concatenate([-sine, sine], axis=1)
    j = jnp.arange(BLOCKS, dtype=jnp.int32)
    y, z, c, half = j // 32, (j // 4) % 8, (j // 2) % 2, j % 2
    kv_place = ((y * 2 + c) * ZS + z) * 2 + half
    q_place = ((c * YS + y) * ZS + z) * 2 + half
    holds = old_block[None, :] == j[:, None]
    kv_block = jnp.sum(jnp.where(holds, kv_place[None, :], 0), axis=1)
    q_block = jnp.sum(jnp.where(holds, q_place[None, :], 0), axis=1)
    moved = layer(
        kv_block, q_block, new_block,
        queries.reshape(64, LOCAL, DIM), keys_values.reshape(2, 8, LOCAL, DIM), cos, sin,
    )
    return moved.reshape(queries.shape)


def solution(mesh):
    return jax.shard_map(
        per_device,
        mesh=mesh,
        in_specs=(P("pp", None, None, "cp", None), P("pp", None, None, None, "cp", None), P(), P()),
        out_specs=P("pp", None, None, "cp", None),
        check_vma=False,
    )
```

```python
import math

import jax
import jax.numpy as jnp
from jax import lax
from jax.experimental import pallas as pl
from jax.experimental.pallas import tpu as pltpu
from jax.sharding import PartitionSpec as P

MESH = pl.DeviceIdType.MESH
F32 = jnp.float32
BF16 = jnp.bfloat16
LENGTH = 4096
DIM = 128
BLOCKS = 128
ROWS = 32
LOCAL = 64
YS, ZS = 4, 8
CHIPS = YS * ZS
SECTIONS = 8
VROWS = 144
TILE = 1024
TB = TILE // ROWS
Z_ORDER = (1, 7, 3, 5, 2, 6, 4)
ODD, EVEN = (1, 7, 3, 5), (2, 6, 4, 0)


def turned(x, cos, sin):
    wide = x.astype(F32)
    return (wide * cos + pltpu.roll(wide, 64, wide.ndim - 1) * sin).astype(BF16)


def layer_kernel(
    kv_block, q_block, new_block, q_ref, kv_ref, cos_ref, sin_ref, o_ref,
    qs, qz, qa, qb, kvs, kz, okv, oa, ob, ra, rb, oz, k2, vt, seq, qt, acc, mx, sent, got, loc,
):
    pp = lax.axis_index("pp")
    me = lax.axis_index("cp")
    y, z, c = me // 16, lax.rem(me // 2, ZS), lax.rem(me, 2)
    ahead, behind = lax.rem(pp + 1, SECTIONS), lax.rem(pp + SECTIONS - 1, SECTIONS)
    other = 1 - c
    parity = lax.rem(z, 2)
    sign = 1 - 2 * c

    def along_z(dz):
        return lax.rem(z + sign * dz + ZS, ZS)

    def along_y(dy):
        return lax.rem(y + sign * dy + YS, YS)

    def device(at_y, at_z, core=c):
        return (at_y * ZS + at_z) * 2 + core

    barrier = pltpu.get_barrier_semaphore()
    greeted = [(pp, device(y, along_z(dz))) for dz in range(1, ZS)]
    greeted += [(pp, device(along_y(dy), z)) for dy in range(1, YS)]
    greeted += [(pp, device(y, z, other))]
    greeted += [(behind, device(along_y(dy), z)) for dy in range(YS)]
    for place in greeted:
        pl.semaphore_signal(barrier, inc=1, device_id=place, device_id_type=MESH)

    cos, sin = cos_ref[...], sin_ref[...]

    def turn_keys(j, carry):
        kvs[0, j] = turned(kv_ref[0, j], cos, sin).reshape(2, ROWS, DIM)
        kvs[1, j] = kv_ref[1, j].reshape(2, ROWS, DIM)
        return carry

    lax.fori_loop(0, 8, turn_keys, 0)
    pl.semaphore_wait(barrier, len(greeted))

    count = [0, 0]

    def remote(src, dst, dev, section=pp):
        copy = pltpu.make_async_remote_copy(
            src_ref=src, dst_ref=dst, send_sem=sent.at[count[0]], recv_sem=got.at[count[0]],
            device_id=(section, dev), device_id_type=MESH,
        )
        count[0] += 1
        copy.start()
        return copy

    def local(src, dst):
        copy = pltpu.make_async_copy(src, dst, loc.at[count[1]])
        count[1] += 1
        copy.start()
        return copy

    outgoing = []

    ky = [
        remote(kvs.at[:, pl.ds(2 * along_y(dy), 2)], kz.at[:, :, pl.ds(2 * y, 2)], device(along_y(dy), z))
        for dy in (2, 1, 3)
    ]
    ky_own = local(kvs.at[:, pl.ds(2 * y, 2)], kz.at[:, :, pl.ds(2 * y, 2)])

    held = (qa, qb)

    def turn_queries(head, at_z, out):
        def one(at_y, carry):
            item = (2 * at_y + lax.rem(at_z, 2)) * 8 + (at_z // 2) * 2 + head
            out[at_y] = turned(q_ref[item], cos, sin).reshape(2, ROWS, DIM)
            return carry

        lax.fori_loop(0, YS, one, 0, unroll=True)

    def queries_along_z(head):
        copies = {}
        for dz in Z_ORDER:
            to = along_z(dz)
            turn_queries(head, to, qs.at[head, to])
            copies[dz] = remote(qs.at[head, to], qz.at[head, parity, z // 2], device(y, to))
        turn_queries(head, z, qz.at[head, parity, z // 2])
        return copies

    def queries_along_y(head, steps, copies):
        which = lax.rem(parity + steps[0], 2)
        for dz in steps:
            if dz:
                copies[dz].wait_recv()
        place = held[head].at[pl.ds((c * YS + y) * ZS + which * 4, 4)]
        return [
            remote(qz.at[head, which, :, along_y(dy)], place, device(along_y(dy), z)) for dy in (2, 1, 3)
        ], local(qz.at[head, which, :, y], place)

    za = queries_along_z(0)
    for copy in ky:
        copy.wait_recv()
    ky_own.wait()

    def part(at_z, half=None):
        block = c * ZS + at_z
        return okv.at[:, block] if half is None else okv.at[half, block]

    def near(dz):
        return remote(kz.at[:, lax.rem(parity + dz, 2)], part(z), device(y, along_z(dz)))

    def pass_on(came, to, half=None):
        ref = part(along_z(came), half)
        return remote(ref, ref, device(y, along_z(to)))

    one_up, one_down = near(1), near(7)
    two_up, two_down = near(2), near(6)
    kz_own = local(kz.at[:, parity], part(z))
    one_up.wait_recv()
    three_up = pass_on(7, 2)
    one_down.wait_recv()
    three_down = pass_on(1, 6)
    zb = queries_along_z(1)
    ya, ya_own = queries_along_y(0, ODD, za)
    two_up.wait_recv()
    four_up = pass_on(6, 2, 0)
    two_down.wait_recv()
    four_down = pass_on(2, 6, 1)
    more, more_own = queries_along_y(0, EVEN, za)
    ya += more
    for copy in (three_up, three_down, four_up, four_down):
        copy.wait_recv()
    kz_own.wait()
    half_kv = okv.at[:, pl.ds(c * ZS, ZS)]
    kv_swap = remote(half_kv, half_kv, device(y, z, other))
    for copy in ya:
        copy.wait_recv()
    ya_own.wait()
    more_own.wait()

    def swap_queries(head):
        half_q = held[head].at[pl.ds(c * CHIPS, CHIPS)]
        return remote(half_q, half_q, device(y, z, other))

    q_swap = swap_queries(0)
    kv_swap.wait()
    outgoing += ky + list(za.values()) + list(zb.values()) + ya
    outgoing += [one_up, one_down, two_up, two_down, three_up, three_down, four_up, four_down]

    def arrange(b, carry):
        dst = pl.ds(pl.multiple_of(b * ROWS, ROWS), ROWS)
        at = kv_block[b]
        keys = okv[0, at // 8, lax.rem(at, 8)]
        k2[dst, 0:DIM] = keys
        k2[dst, DIM : 2 * DIM] = keys
        seq[dst, :] = okv[1, at // 8, lax.rem(at, 8)]
        return carry

    lax.fori_loop(0, BLOCKS, arrange, 0, unroll=8)
    for j in range(LENGTH // 512):
        vt[0:DIM, j * 512 : (j + 1) * 512] = seq[j * 512 : (j + 1) * 512, :].T
    vt[DIM:VROWS, :] = jnp.ones((VROWS - DIM, LENGTH), BF16)

    scale = math.log2(math.e) / math.sqrt(DIM)
    tiles = (c, 3 - c)

    def attend(head, out, between):
        t_copies = []
        for slot in range(2):
            tile = tiles[slot]

            def pick(b, carry):
                at = q_block[tile * TB + b]
                seq[pl.ds(pl.multiple_of(b * ROWS, ROWS), ROWS), :] = held[head][at // 2, lax.rem(at, 2)]
                return carry

            lax.fori_loop(0, TB, pick, 0, unroll=8)
            for j in range(TILE // 512):
                cols = slice(j * 512, (j + 1) * 512)
                x = seq[cols, :].astype(F32) * scale
                high = x.astype(BF16)
                low = (x - high.astype(F32)).astype(BF16)
                qt[0:DIM, cols] = high.T
                qt[DIM : 2 * DIM, cols] = low.T

            def block(k0, first):
                s = jnp.dot(k2[pl.ds(k0, TILE), :], qt[...], preferred_element_type=F32)
                if first:
                    key = lax.broadcasted_iota(jnp.int32, s.shape, 0)
                    query = lax.broadcasted_iota(jnp.int32, s.shape, 1)
                    s = jnp.where(key <= query, s, -1e30)
                top = jnp.max(s, axis=0, keepdims=True)
                if not first:
                    before = mx[...]
                    top = jnp.maximum(before, top)
                weights = jnp.exp2(s - top).astype(BF16)
                summed = jnp.dot(vt[:, pl.ds(k0, TILE)], weights, preferred_element_type=F32)
                if not first:
                    summed = acc[...] * jnp.exp2(before - top) + summed
                acc[...] = summed
                mx[...] = top

            block(pl.multiple_of(tile * TILE, TILE), True)

            def body(j, carry):
                block(pl.multiple_of(j * TILE, TILE), False)
                return carry

            lax.fori_loop(0, tile, body, 0)
            rows = pl.ds(tile * TB, TB)
            out[rows] = (acc[0:DIM, :] / acc[DIM : DIM + 1, :]).T.astype(BF16).reshape(TB, ROWS, DIM)
            done = out.at[rows]
            t_copies.append(remote(done, done, device(y, z, other)))
            if slot == 0:
                between()
        for copy in t_copies:
            copy.wait()

    def hand_on(head, out, relaid):
        def relay(b, carry):
            j = ((lax.rem(b // 2, YS) * ZS + b // 8) * 2 + c) * 2 + lax.rem(b, 2)
            relaid[b // 8, lax.rem(b // 2, YS), lax.rem(b, 2)] = out[new_block[j]]
            return carry

        lax.fori_loop(0, 2 * CHIPS, relay, 0, unroll=8)
        copies = {}
        for dz in Z_ORDER:
            to = along_z(dz)
            copies[dz] = remote(relaid.at[to], oz.at[head, parity, z // 2], device(y, to))
        return copies, local(relaid.at[z], oz.at[head, parity, z // 2])

    def to_next(head, steps, copies, own):
        which = lax.rem(parity + steps[0], 2)
        for dz in steps:
            if dz:
                copies[dz].wait_recv()
            else:
                own.wait()
        return [
            remote(
                oz.at[head, which, :, along_y(dy)], o_ref.at[y, which, :, head],
                device(along_y(dy), z), ahead,
            )
            for dy in (1, 3, 2, 0)
        ]

    yb, yb_own = queries_along_y(1, ODD, zb)
    more, more_own = queries_along_y(1, EVEN, zb)
    yb += more
    outgoing += yb
    q_swap.wait()
    attend(0, oa, lambda: None)
    oza, oza_own = hand_on(0, oa, ra)
    for copy in yb:
        copy.wait_recv()
    yb_own.wait()
    more_own.wait()
    q_swap = swap_queries(1)
    q_swap.wait()
    final = []

    def first_to_next():
        final.extend(to_next(0, ODD, oza, oza_own))
        final.extend(to_next(0, EVEN, oza, oza_own))

    attend(1, ob, first_to_next)
    ozb, ozb_own = hand_on(1, ob, rb)
    final += to_next(1, ODD, ozb, ozb_own)
    final += to_next(1, EVEN, ozb, ozb_own)
    outgoing += list(oza.values()) + list(ozb.values())
    for copy in outgoing:
        copy.wait_send()
    for copy in final:
        copy.wait()


def layer(kv_block, q_block, new_block, queries, pairs, cos, sin):
    vmem = pl.BlockSpec(memory_space=pltpu.VMEM)
    smem = pl.BlockSpec(memory_space=pltpu.SMEM)
    dma = pltpu.SemaphoreType.DMA
    buf = pltpu.VMEM
    return pl.pallas_call(
        layer_kernel,
        out_shape=jax.ShapeDtypeStruct((YS, 2, 4, 2, 2, ROWS, DIM), BF16),
        in_specs=[smem] * 3 + [vmem] * 4,
        out_specs=pl.BlockSpec(memory_space=pl.ANY),
        scratch_shapes=[
            buf((2, ZS, YS, 2, ROWS, DIM), BF16),
            buf((2, 2, 4, YS, 2, ROWS, DIM), BF16),
            buf((64, 2, ROWS, DIM), BF16),
            buf((64, 2, ROWS, DIM), BF16),
            buf((2, 8, 2, ROWS, DIM), BF16),
            buf((2, 2, 8, ROWS, DIM), BF16),
            buf((2, 16, 8, ROWS, DIM), BF16),
            buf((BLOCKS, ROWS, DIM), BF16),
            buf((BLOCKS, ROWS, DIM), BF16),
            buf((ZS, YS, 2, ROWS, DIM), BF16),
            buf((ZS, YS, 2, ROWS, DIM), BF16),
            buf((2, 2, 4, YS, 2, ROWS, DIM), BF16),
            buf((LENGTH, 2 * DIM), BF16),
            buf((VROWS, LENGTH), BF16),
            buf((LENGTH, DIM), BF16),
            buf((2 * DIM, TILE), BF16),
            buf((VROWS, TILE), F32),
            buf((1, TILE), F32),
            dma((80,)), dma((80,)), dma((10,)),
        ],
        compiler_params=pltpu.CompilerParams(
            collective_id=1, has_side_effects=True, vmem_limit_bytes=50 * 2**20
        ),
        name="layer",
    )(kv_block, q_block, new_block, queries, pairs, cos, sin)


def per_device(queries, keys_values, old_block, new_block):
    me = lax.axis_index("cp")
    two = lax.dynamic_slice_in_dim(old_block, me * 2, 2)
    token = (two[:, None] * ROWS + jnp.arange(ROWS, dtype=jnp.int32)[None, :]).reshape(LOCAL)
    spacing = jnp.arange(DIM // 2, dtype=F32) * (2.0 / DIM)
    inverse = jnp.exp(-spacing * jnp.log(F32(1000000.0)))
    angles = token.astype(F32)[:, None] * inverse[None, :]
    cosine, sine = jnp.cos(angles), jnp.sin(angles)
    cos = jnp.concatenate([cosine, cosine], axis=1)
    sin = jnp.concatenate([-sine, sine], axis=1)
    j = jnp.arange(BLOCKS, dtype=jnp.int32)
    y, z, c, half = j // 32, (j // 4) % 8, (j // 2) % 2, j % 2
    kv_place = ((c * ZS + z) * YS + y) * 2 + half
    q_place = ((c * YS + y) * ZS + (z % 2) * 4 + z // 2) * 2 + half
    holds = old_block[None, :] == j[:, None]
    kv_block = jnp.sum(jnp.where(holds, kv_place[None, :], 0), axis=1)
    q_block = jnp.sum(jnp.where(holds, q_place[None, :], 0), axis=1)
    moved = layer(
        kv_block, q_block, new_block,
        queries.reshape(64, LOCAL, DIM), keys_values.reshape(2, 8, LOCAL, DIM), cos, sin,
    )
    return moved.reshape(queries.shape)


def solution(mesh):
    return jax.shard_map(
        per_device,
        mesh=mesh,
        in_specs=(P("pp", None, None, "cp", None), P("pp", None, None, None, "cp", None), P(), P()),
        out_specs=P("pp", None, None, "cp", None),
        check_vma=False,
    )
```

```python
import math
import random

import jax
import jax.numpy as jnp
from jax import lax
from jax.experimental import pallas as pl
from jax.experimental.pallas import tpu as pltpu
from jax.sharding import PartitionSpec as P

MESH = pl.DeviceIdType.MESH
F32 = jnp.float32
BF16 = jnp.bfloat16
LENGTH = 4096
DIM = 128
BLOCKS = 128
ROWS = 32
LOCAL = 64
YS, ZS = 4, 8
CHIPS = YS * ZS
SECTIONS = 8
VROWS = 144
TILE = 1024
TB = TILE // ROWS
PARTS = 2
WIDE = TILE // PARTS
Z_ORDER = (1, 7, 3, 5, 2, 6, 4)
ODD, EVEN = (1, 7, 3, 5), (2, 6, 4, 0)


def steps_of(seed):
    rest = [(dy, dz) for dy in range(YS) for dz in range(ZS)]
    random.Random(seed).shuffle(rest)
    hops_y = {0: 0, 1: 2, 2: 4, 3: 2}
    total, order = [0, 0], []
    while rest:
        share = 64 * (len(order) + 1) / 32

        def cost(step):
            along_z = total[0] + min(step[1], ZS - step[1])
            along_y = total[1] + hops_y[step[0]]
            return (along_z - share) ** 2 + (along_y - share) ** 2

        best = min(rest, key=cost)
        rest.remove(best)
        order.append(best)
        total[0] += min(best[1], ZS - best[1])
        total[1] += hops_y[best[0]]
    return order


def turned(x, cos, sin):
    wide = x.astype(F32)
    return (wide * cos + pltpu.roll(wide, 64, wide.ndim - 1) * sin).astype(BF16)


def layer_kernel(
    old_block, new_block, old_ref, q_hbm, kv_hbm, o_ref,
    q_ref, kv_ref, table, kv_block, q_block, qs, qz, qa, qb, kvs, kz, okv, oa, ob, ra, rb, k2, vt, seq, qt, acc, mx, sent, got, loc, ready,
):
    pp = lax.axis_index("pp")
    me = lax.axis_index("cp")
    y, z, c = me // 16, lax.rem(me // 2, ZS), lax.rem(me, 2)
    ahead, behind = lax.rem(pp + 1, SECTIONS), lax.rem(pp + SECTIONS - 1, SECTIONS)
    other = 1 - c
    parity = lax.rem(z, 2)
    sign = 1 - 2 * c

    def along_z(dz):
        return lax.rem(z + sign * dz + ZS, ZS)

    def along_y(dy):
        return lax.rem(y + sign * dy + YS, YS)

    def device(at_y, at_z, core=c):
        return (at_y * ZS + at_z) * 2 + core

    load_kv = pltpu.make_async_copy(kv_hbm, kv_ref, loc.at[10])
    load_kv.start()
    load_q = pltpu.make_async_copy(q_hbm, q_ref, loc.at[11])
    load_q.start()
    barrier = pltpu.get_barrier_semaphore()
    greeted = [(pp, device(y, along_z(dz))) for dz in range(1, ZS)]
    greeted += [(pp, device(along_y(dy), z)) for dy in range(1, YS)]
    greeted += [(pp, device(y, z, other))]
    greeted += [(ahead, me)]
    for place in greeted:
        pl.semaphore_signal(barrier, inc=1, device_id=place, device_id_type=MESH)

    lane = lax.broadcasted_iota(jnp.int32, (LOCAL, DIM), 1)
    row = lax.broadcasted_iota(jnp.int32, (LOCAL, DIM), 0)
    block = jnp.where(row < ROWS, old_block[2 * me], old_block[2 * me + 1])
    token = (block * ROWS + lax.rem(row, ROWS)).astype(F32)
    spacing = lax.rem(lane, DIM // 2).astype(F32) * (2.0 / DIM)
    angle = token * jnp.exp(-spacing * math.log(1000000.0))
    cos = jnp.cos(angle)
    sin = jnp.where(lane < DIM // 2, -jnp.sin(angle), jnp.sin(angle))

    j = lax.broadcasted_iota(jnp.int32, (BLOCKS, BLOCKS), 0)
    holds = old_ref[...] == lax.broadcasted_iota(jnp.int32, (BLOCKS, BLOCKS), 1)
    jy, jz, jc, half = j // 32, lax.rem(j // 4, ZS), lax.rem(j // 2, 2), lax.rem(j, 2)
    kv_place = ((jc * ZS + jz) * YS + jy) * 2 + half
    q_place = ((jc * YS + jy) * ZS + lax.rem(jz, 2) * 4 + jz // 2) * 2 + half
    table[0:1, :] = jnp.max(jnp.where(holds, kv_place, 0), axis=0, keepdims=True)
    table[1:2, :] = jnp.max(jnp.where(holds, q_place, 0), axis=0, keepdims=True)
    kv_table = pltpu.make_async_copy(table.at[pl.ds(0, 1)], kv_block, loc.at[12])
    kv_table.start()
    q_table = pltpu.make_async_copy(table.at[pl.ds(1, 1)], q_block, loc.at[13])
    q_table.start()
    load_kv.wait()

    def turn_keys(j, carry):
        kvs[0, j] = turned(kv_ref[0, j], cos, sin).reshape(2, ROWS, DIM)
        kvs[1, j] = kv_ref[1, j].reshape(2, ROWS, DIM)
        return carry

    lax.fori_loop(0, 8, turn_keys, 0)
    kv_table.wait()
    q_table.wait()
    load_q.wait()
    pl.semaphore_wait(barrier, len(greeted))

    count = [0, 0]

    def remote(src, dst, dev, section=pp):
        copy = pltpu.make_async_remote_copy(
            src_ref=src, dst_ref=dst, send_sem=sent.at[count[0]], recv_sem=got.at[count[0]],
            device_id=(section, dev), device_id_type=MESH,
        )
        count[0] += 1
        copy.start()
        return copy

    def local(src, dst):
        copy = pltpu.make_async_copy(src, dst, loc.at[count[1]])
        count[1] += 1
        copy.start()
        return copy

    outgoing = []

    ky = [
        remote(kvs.at[:, pl.ds(2 * along_y(dy), 2)], kz.at[:, :, pl.ds(2 * y, 2)], device(along_y(dy), z))
        for dy in (2, 1, 3)
    ]
    ky_own = local(kvs.at[:, pl.ds(2 * y, 2)], kz.at[:, :, pl.ds(2 * y, 2)])

    held = (qa, qb)

    def turn_queries(head, at_z, out):
        def one(at_y, carry):
            item = (2 * at_y + lax.rem(at_z, 2)) * 8 + (at_z // 2) * 2 + head
            out[at_y] = turned(q_ref[item], cos, sin).reshape(2, ROWS, DIM)
            return carry

        lax.fori_loop(0, YS, one, 0, unroll=True)

    def queries_along_z(head):
        copies = {}
        for dz in Z_ORDER:
            to = along_z(dz)
            turn_queries(head, to, qs.at[head, to])
            copies[dz] = remote(qs.at[head, to], qz.at[head, parity, z // 2], device(y, to))
        turn_queries(head, z, qz.at[head, parity, z // 2])
        return copies

    def queries_along_y(head, steps, copies):
        which = lax.rem(parity + steps[0], 2)
        for dz in steps:
            if dz:
                copies[dz].wait_recv()
        place = held[head].at[pl.ds((c * YS + y) * ZS + which * 4, 4)]
        return [
            remote(qz.at[head, which, :, along_y(dy)], place, device(along_y(dy), z)) for dy in (2, 1, 3)
        ], local(qz.at[head, which, :, y], place)

    za = queries_along_z(0)
    for copy in ky:
        copy.wait_recv()
    ky_own.wait()

    def part(at_z, half=None):
        block = c * ZS + at_z
        return okv.at[:, block] if half is None else okv.at[half, block]

    def near(dz):
        return remote(kz.at[:, lax.rem(parity + dz, 2)], part(z), device(y, along_z(dz)))

    def pass_on(came, to, half=None):
        ref = part(along_z(came), half)
        return remote(ref, ref, device(y, along_z(to)))

    one_up, one_down = near(1), near(7)
    two_up, two_down = near(2), near(6)
    kz_own = local(kz.at[:, parity], part(z))
    one_up.wait_recv()
    three_up = pass_on(7, 2)
    one_down.wait_recv()
    three_down = pass_on(1, 6)
    ya, ya_own = queries_along_y(0, ODD, za)
    two_up.wait_recv()
    four_up = pass_on(6, 2, 0)
    two_down.wait_recv()
    four_down = pass_on(2, 6, 1)
    more, more_own = queries_along_y(0, EVEN, za)
    ya += more
    zb = queries_along_z(1)
    for copy in (three_up, three_down, four_up, four_down):
        copy.wait_recv()
    kz_own.wait()
    half_kv = okv.at[:, pl.ds(c * ZS, ZS)]
    kv_swap = remote(half_kv, half_kv, device(y, z, other))
    for copy in ya:
        copy.wait_recv()
    ya_own.wait()
    more_own.wait()
    pl.semaphore_signal(ready, inc=1, device_id=(behind, me), device_id_type=MESH)

    def swap_queries(head):
        half_q = held[head].at[pl.ds(c * CHIPS, CHIPS)]
        return remote(half_q, half_q, device(y, z, other))

    q_swap = swap_queries(0)
    kv_swap.wait()
    outgoing += ky + list(za.values()) + list(zb.values()) + ya
    outgoing += [one_up, one_down, two_up, two_down, three_up, three_down, four_up, four_down]

    def arrange(b, carry):
        dst = pl.ds(pl.multiple_of(b * ROWS, ROWS), ROWS)
        at = kv_block[0, b]
        keys = okv[0, at // 8, lax.rem(at, 8)]
        k2[dst, 0:DIM] = keys
        k2[dst, DIM : 2 * DIM] = keys
        seq[dst, :] = okv[1, at // 8, lax.rem(at, 8)]
        return carry

    lax.fori_loop(0, BLOCKS, arrange, 0, unroll=8)
    for j in range(LENGTH // 512):
        vt[0:DIM, j * 512 : (j + 1) * 512] = seq[j * 512 : (j + 1) * 512, :].T
    vt[DIM:VROWS, :] = jnp.ones((VROWS - DIM, LENGTH), BF16)

    scale = math.log2(math.e) / math.sqrt(DIM)
    tiles = (c, 3 - c)

    def attend(head, out):
        t_copies = []
        for slot in range(2):
            tile = tiles[slot]

            def pick(b, carry):
                at = q_block[0, tile * TB + b]
                seq[pl.ds(pl.multiple_of(b * ROWS, ROWS), ROWS), :] = held[head][at // 2, lax.rem(at, 2)]
                return carry

            lax.fori_loop(0, TB, pick, 0, unroll=8)
            for j in range(TILE // 512):
                cols = slice(j * 512, (j + 1) * 512)
                x = seq[cols, :].astype(F32) * scale
                high = x.astype(BF16)
                low = (x - high.astype(F32)).astype(BF16)
                qt[0:DIM, cols] = high.T
                qt[DIM : 2 * DIM, cols] = low.T

            def score(k0, part, width):
                keys = k2[pl.ds(k0, width), :]
                return jnp.dot(keys, qt[:, part * WIDE : (part + 1) * WIDE], preferred_element_type=F32)

            def blend(k0, width, weights):
                return jnp.dot(vt[:, pl.ds(k0, width)], weights, preferred_element_type=F32)

            own = pl.multiple_of(tile * TILE, TILE)
            ahead_of = score(own, 0, WIDE)
            for part in range(PARTS):
                s, width = ahead_of, (part + 1) * WIDE
                if part + 1 < PARTS:
                    ahead_of = score(own, part + 1, width + WIDE)
                key = lax.broadcasted_iota(jnp.int32, s.shape, 0)
                query = lax.broadcasted_iota(jnp.int32, s.shape, 1)
                s = jnp.where(key <= query + part * WIDE, s, -1e30)
                top = jnp.max(s, axis=0, keepdims=True)
                cols = slice(part * WIDE, width)
                acc[:, cols] = blend(own, width, jnp.exp2(s - top).astype(BF16))
                mx[:, cols] = top

            def body(j, carry):
                k0 = pl.multiple_of(j * TILE, TILE)
                before, total = mx[...], acc[...]
                ahead_of = score(k0, 0, TILE)
                for part in range(PARTS):
                    s = ahead_of
                    if part + 1 < PARTS:
                        ahead_of = score(k0, part + 1, TILE)
                    cols = slice(part * WIDE, (part + 1) * WIDE)
                    top = jnp.maximum(before[:, cols], jnp.max(s, axis=0, keepdims=True))
                    summed = blend(k0, TILE, jnp.exp2(s - top).astype(BF16))
                    acc[:, cols] = total[:, cols] * jnp.exp2(before[:, cols] - top) + summed
                    mx[:, cols] = top
                return carry

            lax.fori_loop(0, tile, body, 0)
            rows = pl.ds(tile * TB, TB)
            out[rows] = (acc[0:DIM, :] / acc[DIM : DIM + 1, :]).T.astype(BF16).reshape(TB, ROWS, DIM)
            done = out.at[rows]
            t_copies.append(remote(done, done, device(y, z, other)))
        for copy in t_copies:
            copy.wait()

    o_steps = steps_of(2)

    def hand_on(head, out, relaid):
        item = ((y * 2 + parity) * 4 + z // 2) * 2 + head
        copies = []
        for dy, dz in o_steps:
            to_y, to_z = along_y(dy), along_z(dz)
            chip = to_y * ZS + to_z
            for half in range(2):
                relaid[chip, half] = out[new_block[(chip * 2 + c) * 2 + half]]
            copies.append(remote(relaid.at[chip], o_ref.at[item], device(to_y, to_z), ahead))
        return copies

    yb, yb_own = queries_along_y(1, ODD, zb)
    more, more_own = queries_along_y(1, EVEN, zb)
    yb += more
    outgoing += yb
    q_swap.wait()
    attend(0, oa)
    pl.semaphore_wait(ready, 1)
    final = hand_on(0, oa, ra)
    for copy in yb:
        copy.wait_recv()
    yb_own.wait()
    more_own.wait()
    q_swap = swap_queries(1)
    q_swap.wait()
    attend(1, ob)
    final += hand_on(1, ob, rb)
    for copy in outgoing:
        copy.wait_send()
    for copy in final:
        copy.wait()


def layer(old_block, new_block, queries, pairs):
    vmem = pl.BlockSpec(memory_space=pltpu.VMEM)
    smem = pl.BlockSpec(memory_space=pltpu.SMEM)
    hbm = pl.BlockSpec(memory_space=pl.ANY)
    dma = pltpu.SemaphoreType.DMA
    buf = pltpu.VMEM
    return pl.pallas_call(
        layer_kernel,
        out_shape=jax.ShapeDtypeStruct((64, 2, ROWS, DIM), BF16),
        in_specs=[smem, smem, vmem, hbm, hbm],
        out_specs=hbm,
        scratch_shapes=[
            buf((64, LOCAL, DIM), BF16),
            buf((2, 8, LOCAL, DIM), BF16),
            buf((8, BLOCKS), jnp.int32),
            pltpu.SMEM((1, BLOCKS), jnp.int32),
            pltpu.SMEM((1, BLOCKS), jnp.int32),
            buf((2, ZS, YS, 2, ROWS, DIM), BF16),
            buf((2, 2, 4, YS, 2, ROWS, DIM), BF16),
            buf((64, 2, ROWS, DIM), BF16),
            buf((64, 2, ROWS, DIM), BF16),
            buf((2, 8, 2, ROWS, DIM), BF16),
            buf((2, 2, 8, ROWS, DIM), BF16),
            buf((2, 16, 8, ROWS, DIM), BF16),
            buf((BLOCKS, ROWS, DIM), BF16),
            buf((BLOCKS, ROWS, DIM), BF16),
            buf((CHIPS, 2, ROWS, DIM), BF16),
            buf((CHIPS, 2, ROWS, DIM), BF16),
            buf((LENGTH, 2 * DIM), BF16),
            buf((VROWS, LENGTH), BF16),
            buf((LENGTH, DIM), BF16),
            buf((2 * DIM, TILE), BF16),
            buf((VROWS, TILE), F32),
            buf((1, TILE), F32),
            dma((112,)), dma((112,)), dma((14,)), pltpu.SemaphoreType.REGULAR,
        ],
        compiler_params=pltpu.CompilerParams(
            collective_id=1, has_side_effects=True, vmem_limit_bytes=50 * 2**20
        ),
        name="layer",
    )(old_block, new_block, old_block[:, None], queries, pairs)


def per_device(queries, keys_values, old_block, new_block):
    moved = layer(
        old_block, new_block, queries.reshape(64, LOCAL, DIM), keys_values.reshape(2, 8, LOCAL, DIM)
    )
    return moved.reshape(queries.shape)


def solution(mesh):
    return jax.shard_map(
        per_device,
        mesh=mesh,
        in_specs=(P("pp", None, None, "cp", None), P("pp", None, None, None, "cp", None), P(), P()),
        out_specs=P("pp", None, None, "cp", None),
        check_vma=False,
    )
```

```python
import math
import random

import jax
import jax.numpy as jnp
from jax import lax
from jax.experimental import pallas as pl
from jax.experimental.pallas import tpu as pltpu
from jax.sharding import PartitionSpec as P

MESH = pl.DeviceIdType.MESH
F32 = jnp.float32
BF16 = jnp.bfloat16
LENGTH = 4096
DIM = 128
BLOCKS = 128
ROWS = 32
LOCAL = 64
YS, ZS = 4, 8
CHIPS = YS * ZS
SECTIONS = 8
VROWS = 144
TILE = 1024
TB = TILE // ROWS
PARTS = 2
WIDE = TILE // PARTS
Z_ORDER = (1, 7, 3, 5, 2, 6, 4)
ODD, EVEN = (1, 7, 3, 5), (2, 6, 4, 0)


def steps_of(seed):
    rest = [(dy, dz) for dy in range(YS) for dz in range(ZS)]
    random.Random(seed).shuffle(rest)
    hops_y = {0: 0, 1: 2, 2: 4, 3: 2}
    total, order = [0, 0], []
    while rest:
        share = 64 * (len(order) + 1) / 32

        def cost(step):
            along_z = total[0] + min(step[1], ZS - step[1])
            along_y = total[1] + hops_y[step[0]]
            return (along_z - share) ** 2 + (along_y - share) ** 2

        best = min(rest, key=cost)
        rest.remove(best)
        order.append(best)
        total[0] += min(best[1], ZS - best[1])
        total[1] += hops_y[best[0]]
    return order


def turned(x, cos, sin):
    wide = x.astype(F32)
    return (wide * cos + pltpu.roll(wide, 64, wide.ndim - 1) * sin).astype(BF16)


def layer_kernel(
    old_block, new_block, old_ref, q_hbm, kv_hbm, o_ref,
    q_ref, kv_ref, table, kv_block, q_block, qs, qz, qa, qb, kvs, kz, okv, oa, ob, ra, rb, k2, vt, seq, qt, acc, mx, sent, got, loc, ready,
):
    pp = lax.axis_index("pp")
    me = lax.axis_index("cp")
    y, z, c = me // 16, lax.rem(me // 2, ZS), lax.rem(me, 2)
    ahead, behind = lax.rem(pp + 1, SECTIONS), lax.rem(pp + SECTIONS - 1, SECTIONS)
    other = 1 - c
    parity = lax.rem(z, 2)
    sign = 1 - 2 * c

    def along_z(dz):
        return lax.rem(z + sign * dz + ZS, ZS)

    def along_y(dy):
        return lax.rem(y + sign * dy + YS, YS)

    def device(at_y, at_z, core=c):
        return (at_y * ZS + at_z) * 2 + core

    load_kv = pltpu.make_async_copy(kv_hbm, kv_ref, loc.at[10])
    load_kv.start()
    load_q = pltpu.make_async_copy(q_hbm, q_ref, loc.at[11])
    load_q.start()
    barrier = pltpu.get_barrier_semaphore()
    greeted = [(pp, device(y, along_z(dz))) for dz in range(1, ZS)]
    greeted += [(pp, device(along_y(dy), z)) for dy in range(1, YS)]
    greeted += [(pp, device(y, z, other))]
    greeted += [(ahead, me)]
    for place in greeted:
        pl.semaphore_signal(barrier, inc=1, device_id=place, device_id_type=MESH)

    lane = lax.broadcasted_iota(jnp.int32, (LOCAL, DIM), 1)
    row = lax.broadcasted_iota(jnp.int32, (LOCAL, DIM), 0)
    block = jnp.where(row < ROWS, old_block[2 * me], old_block[2 * me + 1])
    token = (block * ROWS + lax.rem(row, ROWS)).astype(F32)
    spacing = lax.rem(lane, DIM // 2).astype(F32) * (2.0 / DIM)
    angle = token * jnp.exp(-spacing * math.log(1000000.0))
    cos = jnp.cos(angle)
    sin = jnp.where(lane < DIM // 2, -jnp.sin(angle), jnp.sin(angle))

    j = lax.broadcasted_iota(jnp.int32, (BLOCKS, BLOCKS), 1)
    holds = old_ref[...] == lax.broadcasted_iota(jnp.int32, (BLOCKS, BLOCKS), 0)
    jy, jz, jc, half = j // 32, lax.rem(j // 4, ZS), lax.rem(j // 2, 2), lax.rem(j, 2)
    kv_place = ((jc * ZS + jz) * YS + jy) * 2 + half
    q_place = ((jc * YS + jy) * ZS + lax.rem(jz, 2) * 4 + jz // 2) * 2 + half
    for n, where in enumerate((kv_place, q_place)):
        found = jnp.max(jnp.where(holds, where, 0), axis=1, keepdims=True)
        table[n : n + 1, :] = jnp.broadcast_to(found, (BLOCKS, BLOCKS)).T[0:1, :]
    kv_table = pltpu.make_async_copy(table.at[pl.ds(0, 1)], kv_block, loc.at[12])
    kv_table.start()
    q_table = pltpu.make_async_copy(table.at[pl.ds(1, 1)], q_block, loc.at[13])
    q_table.start()
    load_kv.wait()

    def turn_keys(j, carry):
        kvs[0, j] = turned(kv_ref[0, j], cos, sin).reshape(2, ROWS, DIM)
        kvs[1, j] = kv_ref[1, j].reshape(2, ROWS, DIM)
        return carry

    lax.fori_loop(0, 8, turn_keys, 0)
    kv_table.wait()
    q_table.wait()
    load_q.wait()
    pl.semaphore_wait(barrier, len(greeted))

    count = [0, 0]

    def remote(src, dst, dev, section=pp):
        copy = pltpu.make_async_remote_copy(
            src_ref=src, dst_ref=dst, send_sem=sent.at[count[0]], recv_sem=got.at[count[0]],
            device_id=(section, dev), device_id_type=MESH,
        )
        count[0] += 1
        copy.start()
        return copy

    def local(src, dst):
        copy = pltpu.make_async_copy(src, dst, loc.at[count[1]])
        count[1] += 1
        copy.start()
        return copy

    outgoing = []

    ky = [
        remote(kvs.at[:, pl.ds(2 * along_y(dy), 2)], kz.at[:, :, pl.ds(2 * y, 2)], device(along_y(dy), z))
        for dy in (2, 1, 3)
    ]
    ky_own = local(kvs.at[:, pl.ds(2 * y, 2)], kz.at[:, :, pl.ds(2 * y, 2)])

    held = (qa, qb)

    def turn_queries(head, at_z, out):
        def one(at_y, carry):
            item = (2 * at_y + lax.rem(at_z, 2)) * 8 + (at_z // 2) * 2 + head
            out[at_y] = turned(q_ref[item], cos, sin).reshape(2, ROWS, DIM)
            return carry

        lax.fori_loop(0, YS, one, 0, unroll=True)

    def queries_along_z(head):
        copies = {}
        for dz in Z_ORDER:
            to = along_z(dz)
            turn_queries(head, to, qs.at[head, to])
            copies[dz] = remote(qs.at[head, to], qz.at[head, parity, z // 2], device(y, to))
        turn_queries(head, z, qz.at[head, parity, z // 2])
        return copies

    def queries_along_y(head, steps, copies):
        which = lax.rem(parity + steps[0], 2)
        for dz in steps:
            if dz:
                copies[dz].wait_recv()
        place = held[head].at[pl.ds((c * YS + y) * ZS + which * 4, 4)]
        return [
            remote(qz.at[head, which, :, along_y(dy)], place, device(along_y(dy), z)) for dy in (2, 1, 3)
        ], local(qz.at[head, which, :, y], place)

    za = queries_along_z(0)
    for copy in ky:
        copy.wait_recv()
    ky_own.wait()

    def part(at_z, half=None):
        block = c * ZS + at_z
        return okv.at[:, block] if half is None else okv.at[half, block]

    def near(dz):
        return remote(kz.at[:, lax.rem(parity + dz, 2)], part(z), device(y, along_z(dz)))

    def pass_on(came, to, half=None):
        ref = part(along_z(came), half)
        return remote(ref, ref, device(y, along_z(to)))

    one_up, one_down = near(1), near(7)
    two_up, two_down = near(2), near(6)
    kz_own = local(kz.at[:, parity], part(z))
    one_up.wait_recv()
    three_up = pass_on(7, 2)
    one_down.wait_recv()
    three_down = pass_on(1, 6)
    ya, ya_own = queries_along_y(0, ODD, za)
    two_up.wait_recv()
    four_up = pass_on(6, 2, 0)
    two_down.wait_recv()
    four_down = pass_on(2, 6, 1)
    more, more_own = queries_along_y(0, EVEN, za)
    ya += more
    zb = queries_along_z(1)
    for copy in (three_up, three_down, four_up, four_down):
        copy.wait_recv()
    kz_own.wait()
    half_kv = okv.at[:, pl.ds(c * ZS, ZS)]
    kv_swap = remote(half_kv, half_kv, device(y, z, other))
    for copy in ya:
        copy.wait_recv()
    ya_own.wait()
    more_own.wait()
    pl.semaphore_signal(ready, inc=1, device_id=(behind, me), device_id_type=MESH)

    def swap_queries(head):
        half_q = held[head].at[pl.ds(c * CHIPS, CHIPS)]
        return remote(half_q, half_q, device(y, z, other))

    q_swap = swap_queries(0)
    kv_swap.wait()
    yb, yb_own = queries_along_y(1, ODD, zb)
    outgoing += ky + list(za.values()) + list(zb.values()) + ya
    outgoing += [one_up, one_down, two_up, two_down, three_up, three_down, four_up, four_down]

    def arrange(b, carry):
        dst = pl.ds(pl.multiple_of(b * ROWS, ROWS), ROWS)
        at = kv_block[0, b]
        keys = okv[0, at // 8, lax.rem(at, 8)]
        k2[dst, 0:DIM] = keys
        k2[dst, DIM : 2 * DIM] = keys
        seq[dst, :] = okv[1, at // 8, lax.rem(at, 8)]
        return carry

    lax.fori_loop(0, BLOCKS, arrange, 0, unroll=8)
    for j in range(LENGTH // 512):
        vt[0:DIM, j * 512 : (j + 1) * 512] = seq[j * 512 : (j + 1) * 512, :].T
    vt[DIM:VROWS, :] = jnp.ones((VROWS - DIM, LENGTH), BF16)

    scale = math.log2(math.e) / math.sqrt(DIM)
    tiles = (c, 3 - c)

    def attend(head, out):
        t_copies = []
        for slot in range(2):
            tile = tiles[slot]

            def pick(b, carry):
                at = q_block[0, tile * TB + b]
                seq[pl.ds(pl.multiple_of(b * ROWS, ROWS), ROWS), :] = held[head][at // 2, lax.rem(at, 2)]
                return carry

            lax.fori_loop(0, TB, pick, 0, unroll=8)
            for j in range(TILE // 512):
                cols = slice(j * 512, (j + 1) * 512)
                x = seq[cols, :].astype(F32) * scale
                high = x.astype(BF16)
                low = (x - high.astype(F32)).astype(BF16)
                qt[0:DIM, cols] = high.T
                qt[DIM : 2 * DIM, cols] = low.T

            def score(k0, part, width):
                keys = k2[pl.ds(k0, width), :]
                return jnp.dot(keys, qt[:, part * WIDE : (part + 1) * WIDE], preferred_element_type=F32)

            def blend(k0, width, weights):
                return jnp.dot(vt[:, pl.ds(k0, width)], weights, preferred_element_type=F32)

            own = pl.multiple_of(tile * TILE, TILE)
            ahead_of = score(own, 0, WIDE)
            for part in range(PARTS):
                s, width = ahead_of, (part + 1) * WIDE
                if part + 1 < PARTS:
                    ahead_of = score(own, part + 1, width + WIDE)
                key = lax.broadcasted_iota(jnp.int32, s.shape, 0)
                query = lax.broadcasted_iota(jnp.int32, s.shape, 1)
                s = jnp.where(key <= query + part * WIDE, s, -1e30)
                top = jnp.max(s, axis=0, keepdims=True)
                cols = slice(part * WIDE, width)
                acc[:, cols] = blend(own, width, jnp.exp2(s - top).astype(BF16))
                mx[:, cols] = top

            def body(j, carry):
                k0 = pl.multiple_of(j * TILE, TILE)
                before, total = mx[...], acc[...]
                ahead_of = score(k0, 0, TILE)
                for part in range(PARTS):
                    s = ahead_of
                    if part + 1 < PARTS:
                        ahead_of = score(k0, part + 1, TILE)
                    cols = slice(part * WIDE, (part + 1) * WIDE)
                    top = jnp.maximum(before[:, cols], jnp.max(s, axis=0, keepdims=True))
                    summed = blend(k0, TILE, jnp.exp2(s - top).astype(BF16))
                    acc[:, cols] = total[:, cols] * jnp.exp2(before[:, cols] - top) + summed
                    mx[:, cols] = top
                return carry

            lax.fori_loop(0, tile, body, 0)
            rows = pl.ds(tile * TB, TB)
            out[rows] = (acc[0:DIM, :] / acc[DIM : DIM + 1, :]).T.astype(BF16).reshape(TB, ROWS, DIM)
            done = out.at[rows]
            t_copies.append(remote(done, done, device(y, z, other)))
        for copy in t_copies:
            copy.wait()

    o_steps = steps_of(2)

    def hand_on(head, out, relaid):
        item = ((y * 2 + parity) * 4 + z // 2) * 2 + head
        copies = []
        for dy, dz in o_steps:
            to_y, to_z = along_y(dy), along_z(dz)
            chip = to_y * ZS + to_z
            for half in range(2):
                relaid[chip, half] = out[new_block[(chip * 2 + c) * 2 + half]]
            copies.append(remote(relaid.at[chip], o_ref.at[item], device(to_y, to_z), ahead))
        return copies

    more, more_own = queries_along_y(1, EVEN, zb)
    yb += more
    outgoing += yb
    q_swap.wait()
    attend(0, oa)
    pl.semaphore_wait(ready, 1)
    for copy in yb:
        copy.wait_recv()
    yb_own.wait()
    more_own.wait()
    q_swap = swap_queries(1)
    final = hand_on(0, oa, ra)
    q_swap.wait()
    attend(1, ob)
    final += hand_on(1, ob, rb)
    for copy in outgoing:
        copy.wait_send()
    for copy in final:
        copy.wait()


def layer(old_block, new_block, queries, pairs):
    vmem = pl.BlockSpec(memory_space=pltpu.VMEM)
    smem = pl.BlockSpec(memory_space=pltpu.SMEM)
    hbm = pl.BlockSpec(memory_space=pl.ANY)
    dma = pltpu.SemaphoreType.DMA
    buf = pltpu.VMEM
    return pl.pallas_call(
        layer_kernel,
        out_shape=jax.ShapeDtypeStruct((64, 2, ROWS, DIM), BF16),
        in_specs=[smem, smem, vmem, hbm, hbm],
        out_specs=hbm,
        scratch_shapes=[
            buf((64, LOCAL, DIM), BF16),
            buf((2, 8, LOCAL, DIM), BF16),
            buf((8, BLOCKS), jnp.int32),
            pltpu.SMEM((1, BLOCKS), jnp.int32),
            pltpu.SMEM((1, BLOCKS), jnp.int32),
            buf((2, ZS, YS, 2, ROWS, DIM), BF16),
            buf((2, 2, 4, YS, 2, ROWS, DIM), BF16),
            buf((64, 2, ROWS, DIM), BF16),
            buf((64, 2, ROWS, DIM), BF16),
            buf((2, 8, 2, ROWS, DIM), BF16),
            buf((2, 2, 8, ROWS, DIM), BF16),
            buf((2, 16, 8, ROWS, DIM), BF16),
            buf((BLOCKS, ROWS, DIM), BF16),
            buf((BLOCKS, ROWS, DIM), BF16),
            buf((CHIPS, 2, ROWS, DIM), BF16),
            buf((CHIPS, 2, ROWS, DIM), BF16),
            buf((LENGTH, 2 * DIM), BF16),
            buf((VROWS, LENGTH), BF16),
            buf((LENGTH, DIM), BF16),
            buf((2 * DIM, TILE), BF16),
            buf((VROWS, TILE), F32),
            buf((1, TILE), F32),
            dma((112,)), dma((112,)), dma((14,)), pltpu.SemaphoreType.REGULAR,
        ],
        compiler_params=pltpu.CompilerParams(
            collective_id=1, has_side_effects=True, vmem_limit_bytes=63 * 2**20
        ),
        name="layer",
    )(old_block, new_block, old_block[None, :], queries, pairs)


def per_device(queries, keys_values, old_block, new_block):
    moved = layer(
        old_block, new_block, queries.reshape(64, LOCAL, DIM), keys_values.reshape(2, 8, LOCAL, DIM)
    )
    return moved.reshape(queries.shape)


def solution(mesh):
    return jax.shard_map(
        per_device,
        mesh=mesh,
        in_specs=(P("pp", None, None, "cp", None), P("pp", None, None, None, "cp", None), P(), P()),
        out_specs=P("pp", None, None, "cp", None),
        check_vma=False,
    )
```

```python
import math
import random

import jax
import jax.numpy as jnp
from jax import lax
from jax.experimental import pallas as pl
from jax.experimental.pallas import tpu as pltpu
from jax.sharding import PartitionSpec as P

MESH = pl.DeviceIdType.MESH
F32 = jnp.float32
BF16 = jnp.bfloat16
LENGTH = 4096
DIM = 128
BLOCKS = 128
ROWS = 32
LOCAL = 64
YS, ZS = 4, 8
CHIPS = YS * ZS
SECTIONS = 8
VROWS = 144
TILE = 1024
TB = TILE // ROWS
PARTS = 2
WIDE = TILE // PARTS
Z_ORDER = (1, 7, 3, 5, 2, 6, 4)
ODD, EVEN = (1, 7, 3, 5), (2, 6, 4, 0)


def steps_of(seed):
    rest = [(dy, dz) for dy in range(YS) for dz in range(ZS)]
    random.Random(seed).shuffle(rest)
    hops_y = {0: 0, 1: 2, 2: 4, 3: 2}
    total, order = [0, 0], []
    while rest:
        share = 64 * (len(order) + 1) / 32

        def cost(step):
            along_z = total[0] + min(step[1], ZS - step[1])
            along_y = total[1] + hops_y[step[0]]
            return (along_z - share) ** 2 + (along_y - share) ** 2

        best = min(rest, key=cost)
        rest.remove(best)
        order.append(best)
        total[0] += min(best[1], ZS - best[1])
        total[1] += hops_y[best[0]]
    return order


def turned(x, cos, sin):
    wide = x.astype(F32)
    return (wide * cos + pltpu.roll(wide, 64, wide.ndim - 1) * sin).astype(BF16)


def layer_kernel(
    old_block, new_block, old_ref, q_hbm, kv_hbm, o_ref,
    q_ref, kv_ref, table, kv_block, q_block, qs, qz, qa, qb, kvs, kz, okv, oa, ob, ra, rb, k2, vt, seq, qt, acc, mx, sent, got, loc, ready,
):
    pp = lax.axis_index("pp")
    me = lax.axis_index("cp")
    y, z, c = me // 16, lax.rem(me // 2, ZS), lax.rem(me, 2)
    ahead, behind = lax.rem(pp + 1, SECTIONS), lax.rem(pp + SECTIONS - 1, SECTIONS)
    other = 1 - c
    parity = lax.rem(z, 2)
    sign = 1 - 2 * c

    def along_z(dz):
        return lax.rem(z + sign * dz + ZS, ZS)

    def along_y(dy):
        return lax.rem(y + sign * dy + YS, YS)

    def device(at_y, at_z, core=c):
        return (at_y * ZS + at_z) * 2 + core

    load_kv = pltpu.make_async_copy(kv_hbm, kv_ref, loc.at[10])
    load_kv.start()
    load_q = pltpu.make_async_copy(q_hbm, q_ref, loc.at[11])
    load_q.start()
    barrier = pltpu.get_barrier_semaphore()
    greeted = [(pp, device(y, along_z(dz))) for dz in range(1, ZS)]
    greeted += [(pp, device(along_y(dy), z)) for dy in range(1, YS)]
    greeted += [(pp, device(y, z, other))]
    greeted += [(ahead, me)]
    for place in greeted:
        pl.semaphore_signal(barrier, inc=1, device_id=place, device_id_type=MESH)

    lane = lax.broadcasted_iota(jnp.int32, (LOCAL, DIM), 1)
    row = lax.broadcasted_iota(jnp.int32, (LOCAL, DIM), 0)
    block = jnp.where(row < ROWS, old_block[2 * me], old_block[2 * me + 1])
    token = (block * ROWS + lax.rem(row, ROWS)).astype(F32)
    spacing = lax.rem(lane, DIM // 2).astype(F32) * (2.0 / DIM)
    angle = token * jnp.exp(-spacing * math.log(1000000.0))
    cos = jnp.cos(angle)
    sin = jnp.where(lane < DIM // 2, -jnp.sin(angle), jnp.sin(angle))

    j = lax.broadcasted_iota(jnp.int32, (BLOCKS, BLOCKS), 1)
    holds = old_ref[...] == lax.broadcasted_iota(jnp.int32, (BLOCKS, BLOCKS), 0)
    jy, jz, jc, half = j // 32, lax.rem(j // 4, ZS), lax.rem(j // 2, 2), lax.rem(j, 2)
    kv_place = ((jc * ZS + jz) * YS + jy) * 2 + half
    q_place = ((jc * YS + jy) * ZS + lax.rem(jz, 2) * 4 + jz // 2) * 2 + half
    for n, where in enumerate((kv_place, q_place)):
        found = jnp.max(jnp.where(holds, where, 0), axis=1, keepdims=True)
        table[n : n + 1, :] = jnp.broadcast_to(found, (BLOCKS, BLOCKS)).T[0:1, :]
    kv_table = pltpu.make_async_copy(table.at[pl.ds(0, 1)], kv_block, loc.at[12])
    kv_table.start()
    q_table = pltpu.make_async_copy(table.at[pl.ds(1, 1)], q_block, loc.at[13])
    q_table.start()
    load_kv.wait()

    def turn_keys(j, carry):
        kvs[0, j] = turned(kv_ref[0, j], cos, sin).reshape(2, ROWS, DIM)
        kvs[1, j] = kv_ref[1, j].reshape(2, ROWS, DIM)
        return carry

    lax.fori_loop(0, 8, turn_keys, 0)
    kv_table.wait()
    q_table.wait()
    load_q.wait()
    pl.semaphore_wait(barrier, len(greeted))

    count = [0, 0]

    def remote(src, dst, dev, section=pp):
        copy = pltpu.make_async_remote_copy(
            src_ref=src, dst_ref=dst, send_sem=sent.at[count[0]], recv_sem=got.at[count[0]],
            device_id=(section, dev), device_id_type=MESH,
        )
        count[0] += 1
        copy.start()
        return copy

    def local(src, dst):
        copy = pltpu.make_async_copy(src, dst, loc.at[count[1]])
        count[1] += 1
        copy.start()
        return copy

    outgoing = []

    ky = [
        remote(kvs.at[:, pl.ds(2 * along_y(dy), 2)], kz.at[:, :, pl.ds(2 * y, 2)], device(along_y(dy), z))
        for dy in (2, 1, 3)
    ]
    ky_own = local(kvs.at[:, pl.ds(2 * y, 2)], kz.at[:, :, pl.ds(2 * y, 2)])

    held = (qa, qb)

    def turn_queries(head, at_z, out):
        def one(at_y, carry):
            item = (2 * at_y + lax.rem(at_z, 2)) * 8 + (at_z // 2) * 2 + head
            out[at_y] = turned(q_ref[item], cos, sin).reshape(2, ROWS, DIM)
            return carry

        lax.fori_loop(0, YS, one, 0, unroll=True)

    def queries_along_z(head):
        copies = {}
        for dz in Z_ORDER:
            to = along_z(dz)
            turn_queries(head, to, qs.at[head, to])
            copies[dz] = remote(qs.at[head, to], qz.at[head, parity, z // 2], device(y, to))
        turn_queries(head, z, qz.at[head, parity, z // 2])
        return copies

    def queries_along_y(head, steps, copies):
        which = lax.rem(parity + steps[0], 2)
        for dz in steps:
            if dz:
                copies[dz].wait_recv()
        place = held[head].at[pl.ds((c * YS + y) * ZS + which * 4, 4)]
        return [
            remote(qz.at[head, which, :, along_y(dy)], place, device(along_y(dy), z)) for dy in (2, 1, 3)
        ], local(qz.at[head, which, :, y], place)

    za = queries_along_z(0)
    for copy in ky:
        copy.wait_recv()
    ky_own.wait()

    def part(at_z, half=None):
        block = c * ZS + at_z
        return okv.at[:, block] if half is None else okv.at[half, block]

    def near(dz):
        return remote(kz.at[:, lax.rem(parity + dz, 2)], part(z), device(y, along_z(dz)))

    def pass_on(came, to, half=None):
        ref = part(along_z(came), half)
        return remote(ref, ref, device(y, along_z(to)))

    one_up, one_down = near(1), near(7)
    two_up, two_down = near(2), near(6)
    kz_own = local(kz.at[:, parity], part(z))
    one_up.wait_recv()
    three_up = pass_on(7, 2)
    one_down.wait_recv()
    three_down = pass_on(1, 6)
    ya, ya_own = queries_along_y(0, ODD, za)
    two_up.wait_recv()
    four_up = pass_on(6, 2, 0)
    two_down.wait_recv()
    four_down = pass_on(2, 6, 1)
    more, more_own = queries_along_y(0, EVEN, za)
    ya += more
    zb = queries_along_z(1)
    for copy in (three_up, three_down, four_up, four_down):
        copy.wait_recv()
    kz_own.wait()
    half_kv = okv.at[:, pl.ds(c * ZS, ZS)]
    kv_swap = remote(half_kv, half_kv, device(y, z, other))
    for copy in ya:
        copy.wait_recv()
    ya_own.wait()
    more_own.wait()
    pl.semaphore_signal(ready, inc=1, device_id=(behind, me), device_id_type=MESH)

    def swap_queries(head):
        half_q = held[head].at[pl.ds(c * CHIPS, CHIPS)]
        return remote(half_q, half_q, device(y, z, other))

    q_swap = swap_queries(0)
    kv_swap.wait()
    yb, yb_own = queries_along_y(1, ODD, zb)
    outgoing += ky + list(za.values()) + list(zb.values()) + ya
    outgoing += [one_up, one_down, two_up, two_down, three_up, three_down, four_up, four_down]

    def arrange(b, carry):
        dst = pl.ds(pl.multiple_of(b * ROWS, ROWS), ROWS)
        at = kv_block[0, b]
        keys = okv[0, at // 8, lax.rem(at, 8)]
        k2[dst, 0:DIM] = keys
        k2[dst, DIM : 2 * DIM] = keys
        seq[dst, :] = okv[1, at // 8, lax.rem(at, 8)]
        return carry

    lax.fori_loop(0, BLOCKS, arrange, 0, unroll=8)
    for j in range(LENGTH // 512):
        vt[0:DIM, j * 512 : (j + 1) * 512] = seq[j * 512 : (j + 1) * 512, :].T
    vt[DIM:VROWS, :] = jnp.ones((VROWS - DIM, LENGTH), BF16)

    scale = math.log2(math.e) / math.sqrt(DIM)
    tiles = (c, 3 - c)

    def attend(head, out):
        t_copies = []
        for slot in range(2):
            tile = tiles[slot]

            def pick(b, carry):
                at = q_block[0, tile * TB + b]
                seq[pl.ds(pl.multiple_of(b * ROWS, ROWS), ROWS), :] = held[head][at // 2, lax.rem(at, 2)]
                return carry

            lax.fori_loop(0, TB, pick, 0, unroll=8)
            for j in range(TILE // 512):
                cols = slice(j * 512, (j + 1) * 512)
                x = seq[cols, :].astype(F32) * scale
                high = x.astype(BF16)
                low = (x - high.astype(F32)).astype(BF16)
                qt[0:DIM, cols] = high.T
                qt[DIM : 2 * DIM, cols] = low.T

            def score(k0, part, width):
                keys = k2[pl.ds(k0, width), :]
                return jnp.dot(keys, qt[:, part * WIDE : (part + 1) * WIDE], preferred_element_type=F32)

            def blend(k0, width, weights):
                return jnp.dot(vt[:, pl.ds(k0, width)], weights, preferred_element_type=F32)

            own = pl.multiple_of(tile * TILE, TILE)
            ahead_of = score(own, 0, WIDE)
            for part in range(PARTS):
                s, width = ahead_of, (part + 1) * WIDE
                if part + 1 < PARTS:
                    ahead_of = score(own, part + 1, width + WIDE)
                key = lax.broadcasted_iota(jnp.int32, s.shape, 0)
                query = lax.broadcasted_iota(jnp.int32, s.shape, 1)
                s = jnp.where(key <= query + part * WIDE, s, -1e30)
                top = jnp.max(s, axis=0, keepdims=True)
                cols = slice(part * WIDE, width)
                acc[:, cols] = blend(own, width, jnp.exp2(s - top).astype(BF16))
                mx[:, cols] = top

            def body(j, carry):
                k0 = pl.multiple_of(j * TILE, TILE)
                before, total = mx[...], acc[...]
                ahead_of = score(k0, 0, TILE)
                for part in range(PARTS):
                    s = ahead_of
                    if part + 1 < PARTS:
                        ahead_of = score(k0, part + 1, TILE)
                    cols = slice(part * WIDE, (part + 1) * WIDE)
                    top = jnp.maximum(before[:, cols], jnp.max(s, axis=0, keepdims=True))
                    summed = blend(k0, TILE, jnp.exp2(s - top).astype(BF16))
                    acc[:, cols] = total[:, cols] * jnp.exp2(before[:, cols] - top) + summed
                    mx[:, cols] = top
                return carry

            lax.fori_loop(0, tile, body, 0)
            rows = pl.ds(tile * TB, TB)
            out[rows] = (acc[0:DIM, :] / acc[DIM : DIM + 1, :]).T.astype(BF16).reshape(TB, ROWS, DIM)
            done = out.at[rows]
            t_copies.append(remote(done, done, device(y, z, other)))
        for copy in t_copies:
            copy.wait()

    o_steps = steps_of(2)

    def hand_on(head, out, relaid):
        item = ((y * 2 + parity) * 4 + z // 2) * 2 + head
        copies = []
        for dy, dz in o_steps:
            to_y, to_z = along_y(dy), along_z(dz)
            chip = to_y * ZS + to_z
            for half in range(2):
                relaid[chip, half] = out[new_block[(chip * 2 + c) * 2 + half]]
            copies.append(remote(relaid.at[chip], o_ref.at[item], device(to_y, to_z), ahead))
        return copies

    more, more_own = queries_along_y(1, EVEN, zb)
    yb += more
    outgoing += yb
    q_swap.wait()
    attend(0, oa)
    pl.semaphore_wait(ready, 1)
    for copy in yb:
        copy.wait_recv()
    yb_own.wait()
    more_own.wait()
    q_swap = swap_queries(1)
    final = hand_on(0, oa, ra)
    q_swap.wait()
    attend(1, ob)
    final += hand_on(1, ob, rb)
    for copy in outgoing:
        copy.wait_send()
    for copy in final:
        copy.wait()


def layer(old_block, new_block, queries, pairs):
    vmem = pl.BlockSpec(memory_space=pltpu.VMEM)
    smem = pl.BlockSpec(memory_space=pltpu.SMEM)
    hbm = pl.BlockSpec(memory_space=pl.ANY)
    dma = pltpu.SemaphoreType.DMA
    buf = pltpu.VMEM
    return pl.pallas_call(
        layer_kernel,
        out_shape=jax.ShapeDtypeStruct((64, 2, ROWS, DIM), BF16),
        in_specs=[smem, smem, vmem, hbm, hbm],
        out_specs=hbm,
        scratch_shapes=[
            buf((64, LOCAL, DIM), BF16),
            buf((2, 8, LOCAL, DIM), BF16),
            buf((8, BLOCKS), jnp.int32),
            pltpu.SMEM((1, BLOCKS), jnp.int32),
            pltpu.SMEM((1, BLOCKS), jnp.int32),
            buf((2, ZS, YS, 2, ROWS, DIM), BF16),
            buf((2, 2, 4, YS, 2, ROWS, DIM), BF16),
            buf((64, 2, ROWS, DIM), BF16),
            buf((64, 2, ROWS, DIM), BF16),
            buf((2, 8, 2, ROWS, DIM), BF16),
            buf((2, 2, 8, ROWS, DIM), BF16),
            buf((2, 16, 8, ROWS, DIM), BF16),
            buf((BLOCKS, ROWS, DIM), BF16),
            buf((BLOCKS, ROWS, DIM), BF16),
            buf((CHIPS, 2, ROWS, DIM), BF16),
            buf((CHIPS, 2, ROWS, DIM), BF16),
            buf((LENGTH, 2 * DIM), BF16),
            buf((VROWS, LENGTH), BF16),
            buf((LENGTH, DIM), BF16),
            buf((2 * DIM, TILE), BF16),
            buf((VROWS, TILE), F32),
            buf((1, TILE), F32),
            dma((112,)), dma((112,)), dma((14,)), pltpu.SemaphoreType.REGULAR,
        ],
        compiler_params=pltpu.CompilerParams(
            collective_id=1, has_side_effects=True, vmem_limit_bytes=62 * 2**20
        ),
        name="layer",
    )(old_block, new_block, old_block[None, :], queries, pairs)


def per_device(queries, keys_values, old_block, new_block):
    moved = layer(
        old_block, new_block, queries.reshape(64, LOCAL, DIM), keys_values.reshape(2, 8, LOCAL, DIM)
    )
    return moved.reshape(queries.shape)


def solution(mesh):
    return jax.shard_map(
        per_device,
        mesh=mesh,
        in_specs=(P("pp", None, None, "cp", None), P("pp", None, None, None, "cp", None), P(), P()),
        out_specs=P("pp", None, None, "cp", None),
        check_vma=False,
    )
```
